256 devices in a mesh: grid: 32 (over y_lo, z, core), orb: 4 (over x), tau: 2 (over y_hi).
Axes of the slice: x: 4, y: 4 (y_hi: 2, y_lo: 2; y = y_hi * 2 + y_lo), z: 8, core: 2. Of those that a mesh axis runs over, the one named last changes fastest.
Arguments:
- green: bfloat16 [2, 6016, 6016], P('tau', 'grid', 'orb'), may hold values from -0.0009765625 to 0.0009765625
- colloc: bfloat16 [6016, 2048], P('grid', 'orb'), may hold values from -6 to 6
- core: bfloat16 [2048, 2048], P('grid', 'orb'), may hold values from -0.125 to 0.125
Outputs:
- sigma: bfloat16 [2, 6016, 6016], P('tau', 'grid', 'orb')
The draws below stay inside these ranges and needn't reach their ends.
All inputs are finite; a program needn't handle non-finite values.
Results may differ from the reference program's by a relative error of at most 0.025.
Values may be sent and summed in bfloat16 or wider, within the bound.
No kernel may reach another device: no remote copies, remote signals or barrier semaphores. Data moves between devices by JAX's collectives and lax.ppermute only.
A program may use at most 64 MiB of HBM per device.

```python
import jax
import jax.numpy as jnp

NORB = 6016
NGRID = 2048
NTAU = 2


def block_scale(rng, shape, split, smallest, high):
    def one(dim, blocks):
        heights = jax.random.uniform(jax.random.fold_in(jax.random.fold_in(rng, 6), dim), (blocks,), jnp.float32, smallest / len(split), high / len(split))
        return jnp.repeat(jnp.exp(heights), shape[dim] // blocks).reshape((-1,) + (1,) * (len(shape) - dim - 1))

    gain = one(*split[0])
    for cut in split[1:]:
        gain = gain * one(*cut)
    return gain


def bell_draw(key, extent, deviation, most, split=(), dtype=jnp.bfloat16):
    array = jax.random.normal(key, extent, jnp.float32) * deviation
    if len(split) > 0:
        array = block_scale(key, extent, split, -0.22, 0.18) * array
    return jnp.clip(array, min=-most, max=most).astype(dtype)


def setup_inputs(seed: int = 0) -> dict:
    splits = jax.random.split(jax.random.key(seed), 4)
    return {
        "green": bell_draw(splits[0], (NTAU, NORB, NORB), (NORB * NORB) ** -0.5, 0.0009765625, ((0, 2), (1, 32), (2, 4))),
        "colloc": bell_draw(splits[1], (NORB, NGRID), 1.0, 6.0, ((0, 32), (1, 4))),
        "core": bell_draw(splits[2], (NGRID, NGRID), NGRID ** -0.5, 0.125, ((0, 32), (1, 4))),
    }


def reference(green, colloc, core):
    grids = []
    for t in range(2):
        inner = jnp.dot(green[t], colloc, preferred_element_type=jnp.float32).astype(jnp.bfloat16)
        grids.append(jnp.dot(colloc.T, inner, preferred_element_type=jnp.float32).astype(jnp.bfloat16))
    results = []
    for t in range(2):
        pair = (grids[t].astype(jnp.float32) * grids[1 - t].astype(jnp.float32)).astype(jnp.bfloat16)
        left = jnp.dot(pair, core, preferred_element_type=jnp.float32).astype(jnp.bfloat16)
        screened = jnp.dot(core, left, preferred_element_type=jnp.float32)
        kernel = (grids[t].astype(jnp.float32) * screened).astype(jnp.bfloat16)
        half = jnp.dot(colloc, kernel, preferred_element_type=jnp.float32).astype(jnp.bfloat16)
        full = jnp.dot(half, colloc.T, preferred_element_type=jnp.float32)
        results.append((full * (-1.0 / NGRID)).astype(jnp.bfloat16))
    return jnp.stack(results, axis=0)
```

```python
import jax
import jax.numpy as jnp
from jax import lax
from jax.sharding import Mesh
from jax.sharding import PartitionSpec as P

GRID = ("yl", "z", "c")
BF = jnp.bfloat16
F32 = jnp.float32


def swap(value, axes):
    return lax.all_to_all(value, axes, 0, 0, tiled=True)


def spread(value, axes):
    n = lax.axis_size(axes)
    return swap(jnp.broadcast_to(value[None], (n,) + value.shape), axes)


def shift(value, axis, by):
    n = lax.axis_size(axis)
    return lax.ppermute(value, axis, [(i, (i + by) % n) for i in range(n)])


def dot(a, b, ca, cb):
    return lax.dot_general(a, b, (((ca,), (cb,)), ((), ())), preferred_element_type=F32)


def local(green, colloc, core):
    nc, nx = lax.axis_size("c"), lax.axis_size("orb")
    c, x, tau = lax.axis_index("c"), lax.axis_index("orb"), lax.axis_index("tau")
    rows, cols = colloc.shape
    pad = 192
    half_cols = cols // 2
    quarter = cols // 4

    tile = green[0]
    chips = tile.shape[1] // (2 * rows)
    g0 = jnp.pad(tile.reshape(rows, chips, 2 * rows), ((0, 0), (0, 0), (0, 2 * pad - 2 * rows)))
    g0 = g0.reshape(rows, chips * 2 * pad)
    gs = [g0] + [shift(g0, "orb", d) for d in range(1, nx)]

    xpad = jnp.pad(colloc, ((0, pad - rows), (0, 0)))
    xrows = lax.all_gather(xpad, ("orb", "yl", "c"), axis=0, tiled=False)
    xrows = xrows.reshape(nx, 4 * pad, cols)
    zcols = lax.all_gather(core, GRID, axis=0, tiled=True)
    ycore = lax.dynamic_slice_in_dim(zcols, (2 * lax.axis_index("c") + lax.axis_index("yl")) * quarter, quarter, 1)
    zrows = lax.all_gather(core, ("yl", "c"), axis=0, tiled=True)
    zr = lax.dynamic_slice_in_dim(zrows, tau * 2 * core.shape[0], 2 * core.shape[0], 0)
    zr = lax.all_gather(zr, "orb", axis=1, tiled=True)

    split = jnp.stack([colloc[:, :half_cols], colloc[:, half_cols:]])
    mine = swap(split, "c").reshape(2 * rows, half_cols)
    mine = jnp.pad(mine, ((0, 2 * pad - 2 * rows), (0, 0)))
    panel = spread(mine, ("yl", "z"))
    panel = panel.reshape(nx, chips * 2 * pad, half_cols)

    gt = [shift(g, "c", 1) for g in gs]
    def inner_of(blocks):
        acc = 0.0
        for d in range(nx):
            acc = acc + dot(blocks[d], lax.dynamic_index_in_dim(panel, (x - d) % nx, 0, keepdims=False), 1, 0)
        return jnp.pad(acc.astype(BF), ((0, pad - rows), (0, 0)))
    own, other = inner_of(gs), inner_of(gt)
    inner = jnp.stack([jnp.where(c == 0, own, other), jnp.where(c == 0, other, own)])
    inner = swap(jnp.stack([inner[:, :, :quarter], inner[:, :, quarter:]]), "yl")
    inner = inner.reshape(4 * pad, quarter)

    part = lax.dot_general(xrows, inner, (((1,), (0,)), ((), ())), preferred_element_type=F32).astype(BF)
    part = part.reshape(2, 8, quarter, quarter)
    got = swap(part.reshape(16, quarter, quarter), ("tau", "z"))
    g = jnp.sum(got.reshape(2, 8, quarter, quarter).astype(F32), axis=1).astype(BF)
    gf = g.astype(F32)
    pair = (gf[0] * gf[1]).astype(BF)
    prow = spread(pair, ("orb", "c", "yl"))
    prow = jnp.transpose(prow, (1, 0, 2)).reshape(quarter, 16 * quarter)
    left = dot(prow, ycore, 1, 0).astype(BF)
    left = spread(left, ("tau", "z")).reshape(16 * quarter, quarter)
    screened = dot(zr, left, 1, 0)
    kern = (gf * screened[None]).astype(BF)
    send = jnp.broadcast_to(kern[:, None], (2, 8, quarter, quarter)).reshape(16, quarter, quarter)
    kt = swap(send, ("tau", "z"))
    kt = kt.reshape(nx, cols, quarter)
    half = 0.0
    for o in range(nx):
        half = half + dot(xrows[o], kt[o], 1, 0)
    half = half.astype(BF)
    send = jnp.broadcast_to(half.reshape(1, 2, 2, pad, quarter), (nx, 2, 2, pad, quarter))
    send = jnp.transpose(send, (0, 2, 1, 3, 4)).reshape(16, pad, quarter)
    hrow = swap(send, ("orb", "c", "yl"))
    hrow = jnp.transpose(hrow, (1, 0, 2)).reshape(pad, 16 * quarter)

    xj = swap(panel, "orb")
    xo = shift(xj, "c", 1)
    lo, hi = jnp.where(c == 0, xj, xo), jnp.where(c == 0, xo, xj)
    sig = 0.0
    h4 = hrow.reshape(pad, nx, 2, half_cols)
    for o in range(nx):
        sig = sig + dot(h4[:, o, 0], lo[o], 1, 1) + dot(h4[:, o, 1], hi[o], 1, 1)
    scale = -1.0 / (nx * cols)
    sig = (sig * scale).astype(BF)[:rows].reshape(rows, chips, 2 * pad)[:, :, : 2 * rows]
    return sig.reshape(1, rows, chips * 2 * rows)


def solution(mesh):
    fine = Mesh(mesh.devices.reshape(2, 8, 2, 4, 2), GRID + ("orb", "tau"))
    placed = (P("tau", GRID, "orb"), P(GRID, "orb"), P(GRID, "orb"))
    return jax.shard_map(
        local, mesh=fine, in_specs=placed, out_specs=P("tau", GRID, "orb"), check_vma=False
    )
```

```python
import functools

import jax
import jax.numpy as jnp
from jax import lax
from jax.experimental import pallas as pl
from jax.experimental.pallas import tpu as pltpu
from jax.sharding import Mesh
from jax.sharding import PartitionSpec as P

GRID = ("yl", "z", "c")
BF = jnp.bfloat16
F32 = jnp.float32
VMEM = 56 * 2**20


def swap(value, axes):
    return lax.all_to_all(value, axes, 0, 0, tiled=True)


def spread(value, axes):
    n = lax.axis_size(axes)
    return swap(jnp.broadcast_to(value[None], (n,) + value.shape), axes)


def shift(value, axis, by):
    n = lax.axis_size(axis)
    return lax.ppermute(value, axis, [(i, (i + by) % n) for i in range(n)])


def dot(a, b, ca, cb):
    return lax.dot_general(a, b, (((ca,), (cb,)), ((), ())), preferred_element_type=F32)


def fetch(pairs, sems):
    copies = [pltpu.make_async_copy(s, d, sems.at[i]) for i, (s, d) in enumerate(pairs)]
    for copy in copies:
        copy.start()
    return copies


def ring_places(z, n):
    return [z] + [lax.rem(z - d + n, n) for d in (1, 2, 3, 4)] + [lax.rem(z + d, n) for d in (1, 2, 3)]


def inner_kernel(second, place, own, other, *refs):
    ring, refs = refs[:8], refs[8:]
    if second:
        before, refs = refs[0], refs[1:]
    out, zc, rows_out, xbuf, xsem, osem = refs
    yl, z = place[1], place[3]
    copies = fetch([(r, xbuf.at[p]) for r, p in zip(ring, ring_places(z, 8))], xsem)
    if second:
        for k in range(2):
            out[2 * (1 - yl) + k] = before[k]
    for copy in copies:
        copy.wait()
    rows, width = own.shape[0], out.shape[4]
    store = pltpu.make_async_copy(xbuf.at[:, :, pl.ds(0, rows)], rows_out, osem)
    store.start()
    for k in range(2):
        panel = xbuf[4 * k : 4 * k + 4, :, :rows].reshape(own.shape[1], 2 * width)
        for side, block in enumerate((own, other)):
            term = dot(block[...], panel, 1, 0).astype(BF)
            for part in range(2):
                out[2 * yl + k if second else k, part, side] = term[:, part * width : (part + 1) * width]
    cols = pl.ds(pl.multiple_of(place[4] * width, width), width)
    zc[...] = xbuf[:, :, rows:, cols].reshape(zc.shape)
    store.wait()


def half_kernel(blocks, kt, out):
    pad = out.shape[1]
    for q in range(4):
        acc = None
        for o in range(kt.shape[0]):
            term = dot(blocks[o, q, :pad], kt[o], 1, 0)
            acc = term if acc is None else acc + term
        out[2 * (q % 2) + q // 2] = acc.astype(BF)


ANY = pl.BlockSpec(memory_space=pl.ANY)
SMEM = pl.BlockSpec(memory_space=pltpu.SMEM)
VM = pl.BlockSpec(memory_space=pltpu.VMEM)


def inner_call(place, own, other, ring, before=None):
    rows, k = own.shape
    deep, width = ring[0].shape[1:]
    second = before is not None
    count = 4 if second else 2
    return pl.pallas_call(
        functools.partial(inner_kernel, second),
        out_shape=(
            jax.ShapeDtypeStruct((count, 2, 2, rows, width // 2), BF),
            jax.ShapeDtypeStruct((16 * (deep - rows), width // 2), BF),
            jax.ShapeDtypeStruct((8, 2, rows, width), BF),
        ),
        in_specs=[SMEM, VM, VM] + [ANY] * 8 + [VM] * second,
        out_specs=(VM, VM, ANY),
        scratch_shapes=[
            pltpu.VMEM((8, 2, deep, width), BF),
            pltpu.SemaphoreType.DMA((8,)),
            pltpu.SemaphoreType.DMA,
        ],
        compiler_params=pltpu.CompilerParams(vmem_limit_bytes=VMEM),
        cost_estimate=pl.CostEstimate(flops=8 * rows * k * width, bytes_accessed=6 * 2**20, transcendentals=0),
        name="inner",
    )(place, own, other, *ring, *([before] if second else []))


def half_call(blocks, kt, pad):
    width = kt.shape[2]
    return pl.pallas_call(
        half_kernel,
        out_shape=jax.ShapeDtypeStruct((4, pad, width), BF),
        in_specs=[VM] * 2,
        out_specs=VM,
        compiler_params=pltpu.CompilerParams(vmem_limit_bytes=VMEM),
        cost_estimate=pl.CostEstimate(flops=8 * pad * 2048 * width, bytes_accessed=5 * 2**20, transcendentals=0),
        name="half",
    )(blocks, kt)


def sigma_kernel(scale, rows, place, h, near0, near1, far0, far1, out, buf, sem):
    yl, c = place[1], place[2]
    pairs = []
    for i, x in enumerate((near0, near1, far0, far1)):
        pairs += [(x.at[pl.ds(4 * k, 4)], buf.at[i, k]) for k in range(2)]
    copies = fetch(pairs, sem)
    pad, width = h.shape[1:]
    acc = None
    for i in range(4):
        for k in range(2):
            at = 4 * (2 * (yl if i % 2 == 0 else 1 - yl) + k) + 2 * (c if i < 2 else 1 - c)
            a = jnp.concatenate([h[at], h[at + 1]], axis=1)
            copies[2 * i + k].wait()
            term = dot(a, buf[i, k].reshape(-1, 2 * width), 1, 1)
            acc = term if acc is None else acc + term
    acc = acc * scale
    acc = jnp.concatenate([acc[:, b * pad : b * pad + rows] for b in range(acc.shape[1] // pad)], axis=1)
    out[...] = acc.astype(BF)


def sigma_call(place, h, near, far, rows, scale):
    pad = h.shape[1]
    width = near[0].shape[3]
    return pl.pallas_call(
        functools.partial(sigma_kernel, scale, rows),
        out_shape=jax.ShapeDtypeStruct((pad, 8 * rows), BF),
        in_specs=[SMEM, VM] + [ANY] * 4,
        out_specs=VM,
        scratch_shapes=[pltpu.VMEM((4, 2, 4, 2, pad, width), BF), pltpu.SemaphoreType.DMA((8,))],
        compiler_params=pltpu.CompilerParams(vmem_limit_bytes=VMEM),
        cost_estimate=pl.CostEstimate(flops=128 * pad * pad * width, bytes_accessed=8 * 2**20, transcendentals=0),
        name="sigma",
    )(place, h, *near, *far)


def local(green, colloc, core):
    nx = lax.axis_size("orb")
    c, x, tau, yl, z = (lax.axis_index(a) for a in ("c", "orb", "tau", "yl", "z"))
    place = jnp.stack([x, yl, c, z, yl]).astype(jnp.int32)
    rows, cols = colloc.shape
    pad = 192
    deep = pad + core.shape[0]
    half_cols = cols // 2
    quarter = cols // 4

    xpad = jnp.pad(colloc, ((0, pad - rows), (0, 0)))
    same, cross = [], []
    for i in range(32):
        for o in range(nx):
            to = o * 8 + i % 8
            same.append((i * nx + o, to * nx + i // 8))
            cross.append((i * nx + o, (to ^ 1) * nx + i // 8))

    def halves(value):
        low, high = value[:, :half_cols], value[:, half_cols:]
        return jnp.where(c == 0, low, high), jnp.where(c == 0, high, low)

    stay, go = halves(xpad)
    stay = lax.ppermute(stay, GRID + ("orb",), same)
    go = lax.ppermute(go, GRID + ("orb",), cross)
    zstay, zgo = halves(core)
    zgo = shift(zgo, "c", 1)
    stay, go = jnp.concatenate([stay, zstay]), jnp.concatenate([go, zgo])
    own = jnp.where(c == 0, jnp.stack([stay, go]), jnp.stack([go, stay]))

    tile = green[0]
    blocks = tile.shape[1] // rows
    g_own = jnp.pad(tile.reshape(rows, blocks, rows), ((0, pad - rows), (0, 0), (0, pad - rows)))
    g_own = g_own.reshape(pad, blocks * pad)
    own, g_own = lax.optimization_barrier((own, g_own))
    g_other = shift(g_own, "c", 1)

    one_way, other_way = [(0, 2), (2, 0), (1, 3), (3, 1)], [(0, 3), (3, 0), (1, 2), (2, 1)]

    def across(value, way):
        return lax.ppermute(value, ("yl", "tau"), way)

    up, down, mate_up, mate_down = [own], [own], [], []
    for d in range(4):
        moved = [shift(up[d], "z", 1), across(up[d], one_way)]
        if d > 0:
            moved.append(across(down[d], other_way))
        if d < 3:
            moved.append(shift(down[d], "z", -1))
        moved = lax.optimization_barrier(moved)
        up.append(moved[0])
        mate_up.append(moved[1])
        if d > 0:
            mate_down.append(moved[2])
        if d < 3:
            down.append(moved[-1])
    mate_up.append(across(up[4], other_way))
    ring, mate = up + down[1:], mate_up + mate_down

    tall = jnp.concatenate([xpad, core])
    tall, _ = lax.optimization_barrier((tall, up[2]))
    tall = lax.all_gather(tall, ("orb", "yl", "c"), axis=0, tiled=False)
    tall = tall.reshape(nx, 4, deep, cols)

    inner, zfirst, near0 = inner_call(place, g_own, g_other, ring)
    turned = jnp.stack([x, 1 - yl, c, z, yl]).astype(jnp.int32)
    inner, zsecond, near1 = inner_call(turned, g_own, g_other, mate, inner)
    zcols = jnp.where(yl == 0, jnp.stack([zfirst, zsecond]), jnp.stack([zsecond, zfirst]))
    zcols = zcols.reshape(nx * cols, quarter)
    near = [near0, near1]
    far = [shift(v, "c", 1) for v in near]

    inner = swap(inner.reshape(8, 2, pad, quarter), ("orb", "yl")).reshape(nx, 2, 2, pad, quarter)
    inner = jnp.sum(inner.astype(F32), axis=0).astype(BF)
    inner = jnp.where(c == 0, inner, inner[:, ::-1])
    inner = jnp.pad(inner, ((0, 0), (0, 0), (0, deep - pad), (0, 0))).reshape(4 * deep, quarter)

    stack = tall.reshape(nx, 4 * deep, cols)
    part = lax.dot_general(stack, inner, (((1,), (0,)), ((), ())), preferred_element_type=F32)
    part = part.astype(BF).reshape(16, quarter, quarter)
    got = swap(part, ("tau", "z"))
    g = jnp.sum(got.reshape(2, 8, quarter, quarter).astype(F32), axis=1).astype(BF)
    gf = g.astype(F32)
    pair = (gf[0] * gf[1]).astype(BF)
    prow = spread(pair, ("orb", "c", "yl"))
    prow = jnp.transpose(prow, (1, 0, 2)).reshape(quarter, 16 * quarter)
    left = dot(prow, zcols, 1, 0).astype(BF)
    left = spread(left, ("tau", "z")).reshape(16 * quarter, quarter)
    zr = lax.dynamic_slice_in_dim(tall[:, :, pad:], 2 * tau, 2, 1)
    zr = jnp.transpose(zr, (1, 2, 0, 3)).reshape(quarter, nx * cols)
    screened = dot(zr, left, 1, 0)
    kern = (gf * screened[None]).astype(BF)
    kt = jnp.broadcast_to(kern[:, None], (2, 8, quarter, quarter)).reshape(16, quarter, quarter)
    kt = swap(kt, ("tau", "z")).reshape(nx, cols, quarter)
    half = half_call(tall, kt, pad)
    half = jnp.broadcast_to(half[None], (nx, 4, pad, quarter))
    hrow = swap(half.reshape(16, pad, quarter), ("orb", "c", "yl"))
    return sigma_call(place, hrow, near, far, rows, -1.0 / (nx * cols))[None, :rows]


def solution(mesh):
    fine = Mesh(mesh.devices.reshape(2, 8, 2, 4, 2), GRID + ("orb", "tau"))
    placed = (P("tau", GRID, "orb"), P(GRID, "orb"), P(GRID, "orb"))
    return jax.shard_map(
        local, mesh=fine, in_specs=placed, out_specs=P("tau", GRID, "orb"), check_vma=False
    )
```

```python
import functools

import jax
import jax.numpy as jnp
from jax import lax
from jax.experimental import pallas as pl
from jax.experimental.pallas import tpu as pltpu
from jax.sharding import Mesh
from jax.sharding import PartitionSpec as P

GRID = ("yl", "z", "c")
BF = jnp.bfloat16
F32 = jnp.float32
VMEM = 56 * 2**20


def swap(value, axes):
    return lax.all_to_all(value, axes, 0, 0, tiled=True)


def spread(value, axes):
    n = lax.axis_size(axes)
    return swap(jnp.broadcast_to(value[None], (n,) + value.shape), axes)


def shift(value, axis, by):
    n = lax.axis_size(axis)
    return lax.ppermute(value, axis, [(i, (i + by) % n) for i in range(n)])


def dot(a, b, ca, cb):
    return lax.dot_general(a, b, (((ca,), (cb,)), ((), ())), preferred_element_type=F32)


def fetch(pairs, sems):
    copies = [pltpu.make_async_copy(s, d, sems.at[i]) for i, (s, d) in enumerate(pairs)]
    for copy in copies:
        copy.start()
    return copies


def ring_places(z, n):
    return [z] + [lax.rem(z - d + n, n) for d in (1, 2, 3, 4)] + [lax.rem(z + d, n) for d in (1, 2, 3)]


def slot_of(p, x):
    return jnp.where(lax.div(p, 4) == lax.rem(x, 2), p, 4 * lax.div(p, 4) + 3 - lax.rem(p, 4))


def inner_kernel(second, own, other, *refs):
    ring, refs = refs[:8], refs[8:]
    if second:
        before, refs = refs[0], refs[1:]
    out, zc, rows_out, xbuf, xsem, osem = refs
    x, yl, z = (lax.axis_index(a) for a in ("orb", "yl", "z"))
    of = 1 - yl if second else yl
    copies = fetch([(r, xbuf.at[slot_of(p, x)]) for r, p in zip(ring, ring_places(z, 8))], xsem)
    if second:
        for k in range(2):
            out[2 * yl + k] = before[k]
    for copy in copies:
        copy.wait()
    rows, width = own.shape[0], out.shape[4]
    store = pltpu.make_async_copy(xbuf.at[:, :, pl.ds(0, rows)], rows_out, osem)
    store.start()
    for k in range(2):
        panel = xbuf[4 * k : 4 * k + 4, :, :rows].reshape(own.shape[1], 2 * width)
        for side, block in enumerate((own, other)):
            term = dot(block[...], panel, 1, 0).astype(BF)
            for part in range(2):
                out[2 * of + k if second else k, part, side] = term[:, part * width : (part + 1) * width]
    cols = pl.ds(pl.multiple_of(yl * width, width), width)
    strip = zc.shape[0] // 8
    for p in range(8):
        zc[p * strip : (p + 1) * strip] = xbuf[slot_of(p, x), :, rows:, cols].reshape(strip, width)
    store.wait()


def half_kernel(blocks, kt, out):
    pad = out.shape[1]
    for q in range(4):
        acc = None
        for o in range(kt.shape[0]):
            term = dot(blocks[o, q, :pad], kt[o], 1, 0)
            acc = term if acc is None else acc + term
        for o in range(kt.shape[0]):
            out[4 * o + 2 * (q % 2) + q // 2] = acc.astype(BF)


ANY = pl.BlockSpec(memory_space=pl.ANY)
SMEM = pl.BlockSpec(memory_space=pltpu.SMEM)
VM = pl.BlockSpec(memory_space=pltpu.VMEM)


def inner_call(own, other, ring, before=None):
    rows, k = own.shape
    deep, width = ring[0].shape[1:]
    second = before is not None
    count = 4 if second else 2
    return pl.pallas_call(
        functools.partial(inner_kernel, second),
        out_shape=(
            jax.ShapeDtypeStruct((count, 2, 2, rows, width // 2), BF),
            jax.ShapeDtypeStruct((16 * (deep - rows), width // 2), BF),
            jax.ShapeDtypeStruct((8, 2, rows, width), BF),
        ),
        in_specs=[VM, VM] + [VM] * 8 + [VM] * second,
        out_specs=(VM, VM, ANY),
        scratch_shapes=[
            pltpu.VMEM((8, 2, deep, width), BF),
            pltpu.SemaphoreType.DMA((8,)),
            pltpu.SemaphoreType.DMA,
        ],
        compiler_params=pltpu.CompilerParams(vmem_limit_bytes=VMEM),
        cost_estimate=pl.CostEstimate(flops=8 * rows * k * width, bytes_accessed=6 * 2**20, transcendentals=0),
        name="inner",
    )(own, other, *ring, *([before] if second else []))


def half_call(blocks, kt, pad):
    width = kt.shape[2]
    return pl.pallas_call(
        half_kernel,
        out_shape=jax.ShapeDtypeStruct((16, pad, width), BF),
        in_specs=[VM] * 2,
        out_specs=VM,
        compiler_params=pltpu.CompilerParams(vmem_limit_bytes=VMEM),
        cost_estimate=pl.CostEstimate(flops=8 * pad * 2048 * width, bytes_accessed=5 * 2**20, transcendentals=0),
        name="half",
    )(blocks, kt)


def sigma_kernel(scale, rows, h, near0, near1, far0, far1, out):
    yl, c = lax.axis_index("yl"), lax.axis_index("c")
    pad, width = h.shape[1:]
    acc = None
    for i, x in enumerate((near0, near1, far0, far1)):
        for k in range(2):
            at = 4 * (2 * (yl if i % 2 == 0 else 1 - yl) + k) + 2 * (c if i < 2 else 1 - c)
            a = jnp.concatenate([h[at], h[at + 1]], axis=1)
            term = dot(a, x[4 * k : 4 * k + 4].reshape(-1, 2 * width), 1, 1)
            acc = term if acc is None else acc + term
    acc = acc * scale
    acc = jnp.concatenate([acc[:, b * pad : b * pad + rows] for b in range(acc.shape[1] // pad)], axis=1)
    out[...] = acc.astype(BF)


def sigma_call(h, near, far, rows, scale):
    pad = h.shape[1]
    width = near[0].shape[3]
    return pl.pallas_call(
        functools.partial(sigma_kernel, scale, rows),
        out_shape=jax.ShapeDtypeStruct((pad, 8 * rows), BF),
        in_specs=[VM] * 5,
        out_specs=VM,
        compiler_params=pltpu.CompilerParams(vmem_limit_bytes=VMEM),
        cost_estimate=pl.CostEstimate(flops=128 * pad * pad * width, bytes_accessed=8 * 2**20, transcendentals=0),
        name="sigma",
    )(h, *near, *far)


def local(green, colloc, core):
    nx = lax.axis_size("orb")
    c, x, tau, yl, z = (lax.axis_index(a) for a in ("c", "orb", "tau", "yl", "z"))
    rows, cols = colloc.shape
    pad = 192
    deep = pad + core.shape[0]
    half_cols = cols // 2
    quarter = cols // 4

    xpad = jnp.pad(colloc, ((0, pad - rows), (0, 0)))
    same, cross = [], []
    for i in range(32):
        for o in range(nx):
            a = i % 8
            if (i // 8 - o) % 2:
                a = 2 * (3 - a // 2) + a % 2
            to = o * 8 + a
            same.append((i * nx + o, to * nx + i // 8))
            cross.append((i * nx + o, (to ^ 1) * nx + i // 8))

    def halves(value):
        low, high = value[:, :half_cols], value[:, half_cols:]
        return jnp.where(c == 0, low, high), jnp.where(c == 0, high, low)

    stay, go = halves(xpad)
    stay = lax.ppermute(stay, GRID + ("orb",), same)
    go = lax.ppermute(go, GRID + ("orb",), cross)
    zstay, zgo = halves(core)
    zgo = shift(zgo, "c", 1)
    stay, go = jnp.concatenate([stay, zstay]), jnp.concatenate([go, zgo])
    own = jnp.where(c == 0, jnp.stack([stay, go]), jnp.stack([go, stay]))

    tile = green[0]
    blocks = tile.shape[1] // rows
    g_own = jnp.pad(tile.reshape(rows, blocks, rows), ((0, pad - rows), (0, 0), (0, pad - rows)))
    g_own = g_own.reshape(pad, blocks * pad)
    own, g_own = lax.optimization_barrier((own, g_own))
    g_other = shift(g_own, "c", 1)

    one_way, other_way = [(0, 2), (2, 0), (1, 3), (3, 1)], [(0, 3), (3, 0), (1, 2), (2, 1)]

    def across(value, way):
        return lax.ppermute(value, ("yl", "tau"), way)

    up, down, mate_up, mate_down = [own], [own], [], []
    for d in range(4):
        moved = [shift(up[d], "z", 1), across(up[d], one_way)]
        if d > 0:
            moved.append(across(down[d], other_way))
        if d < 3:
            moved.append(shift(down[d], "z", -1))
        moved = lax.optimization_barrier(moved)
        up.append(moved[0])
        mate_up.append(moved[1])
        if d > 0:
            mate_down.append(moved[2])
        if d < 3:
            down.append(moved[-1])
    mate_up.append(across(up[4], other_way))
    ring, mate = up + down[1:], mate_up + mate_down

    tall = jnp.concatenate([xpad, core])
    tall, _ = lax.optimization_barrier((tall, up[2]))
    tall = lax.all_gather(tall, ("orb", "yl", "c"), axis=0, tiled=False)
    tall = tall.reshape(nx, 4, deep, cols)

    inner, zfirst, near0 = inner_call(g_own, g_other, ring)
    inner, zsecond, near1 = inner_call(g_own, g_other, mate, inner)
    zcols = jnp.where(yl == 0, jnp.stack([zfirst, zsecond]), jnp.stack([zsecond, zfirst]))
    zcols = zcols.reshape(nx * cols, quarter)
    near = [near0, near1]
    far = [shift(v, "c", 1) for v in near]

    inner = swap(inner.reshape(8, 2, pad, quarter), ("orb", "yl")).reshape(nx, 2, 2, pad, quarter)
    inner = jnp.sum(inner.astype(F32), axis=0).astype(BF)
    inner = jnp.where(c == 0, inner, inner[:, ::-1])
    inner = jnp.pad(inner, ((0, 0), (0, 0), (0, deep - pad), (0, 0))).reshape(4 * deep, quarter)

    stack = tall.reshape(nx, 4 * deep, cols)
    part = lax.dot_general(stack, inner, (((1,), (0,)), ((), ())), preferred_element_type=F32)
    part = part.astype(BF).reshape(16, quarter, quarter)
    got = swap(part, ("tau", "z"))
    g = jnp.sum(got.reshape(2, 8, quarter, quarter).astype(F32), axis=1).astype(BF)
    gf = g.astype(F32)
    pair = (gf[0] * gf[1]).astype(BF)
    prow = spread(pair, ("orb", "c", "yl"))
    prow = jnp.transpose(prow, (1, 0, 2)).reshape(quarter, 16 * quarter)
    left = dot(prow, zcols, 1, 0).astype(BF)
    left = spread(left, ("tau", "z")).reshape(16 * quarter, quarter)
    zr = lax.dynamic_slice_in_dim(tall[:, :, pad:], 2 * tau, 2, 1)
    zr = jnp.transpose(zr, (1, 2, 0, 3)).reshape(quarter, nx * cols)
    screened = dot(zr, left, 1, 0)
    kern = (gf * screened[None]).astype(BF)
    kt = jnp.broadcast_to(kern[:, None], (2, 8, quarter, quarter)).reshape(16, quarter, quarter)
    kt = swap(kt, ("tau", "z")).reshape(nx, cols, quarter)
    hrow = swap(half_call(tall, kt, pad), ("orb", "c", "yl"))
    return sigma_call(hrow, near, far, rows, -1.0 / (nx * cols))[None, :rows]


def solution(mesh):
    fine = Mesh(mesh.devices.reshape(2, 8, 2, 4, 2), GRID + ("orb", "tau"))
    placed = (P("tau", GRID, "orb"), P(GRID, "orb"), P(GRID, "orb"))
    return jax.shard_map(
        local, mesh=fine, in_specs=placed, out_specs=P("tau", GRID, "orb"), check_vma=False
    )
```

```python
import functools

import jax
import jax.numpy as jnp
from jax import lax
from jax.experimental import pallas as pl
from jax.experimental.pallas import tpu as pltpu
from jax.sharding import Mesh
from jax.sharding import PartitionSpec as P

GRID = ("yl", "z", "c")
BF = jnp.bfloat16
F32 = jnp.float32
VMEM = 56 * 2**20


def swap(value, axes):
    return lax.all_to_all(value, axes, 0, 0, tiled=True)


def spread(value, axes):
    n = lax.axis_size(axes)
    return swap(jnp.broadcast_to(value[None], (n,) + value.shape), axes)


def shift(value, axis, by):
    n = lax.axis_size(axis)
    return lax.ppermute(value, axis, [(i, (i + by) % n) for i in range(n)])


def dot(a, b, ca, cb):
    return lax.dot_general(a, b, (((ca,), (cb,)), ((), ())), preferred_element_type=F32)


def fetch(pairs, sems):
    copies = [pltpu.make_async_copy(s, d, sems.at[i]) for i, (s, d) in enumerate(pairs)]
    for copy in copies:
        copy.start()
    return copies


def ring_places(z, n):
    return [z] + [lax.rem(z - d + n, n) for d in (1, 2, 3, 4)] + [lax.rem(z + d, n) for d in (1, 2, 3)]


def slot_of(p, x):
    return jnp.where(lax.div(p, 4) == lax.rem(x, 2), p, 4 * lax.div(p, 4) + 3 - lax.rem(p, 4))


def inner_kernel(second, own, other, *refs):
    ring, refs = refs[:8], refs[8:]
    if second:
        before, refs = refs[0], refs[1:]
    out, zc, rows_out, xbuf, xsem, osem = refs
    x, yl, z = (lax.axis_index(a) for a in ("orb", "yl", "z"))
    of = 1 - yl if second else yl
    copies = fetch([(r, xbuf.at[slot_of(p, x)]) for r, p in zip(ring, ring_places(z, 8))], xsem)
    if second:
        for k in range(2):
            out[2 * yl + k] = before[k]
    for copy in copies:
        copy.wait()
    rows, width = own.shape[0], out.shape[4]
    store = pltpu.make_async_copy(xbuf.at[:, :, pl.ds(0, rows)], rows_out, osem)
    store.start()
    for k in range(2):
        panel = xbuf[4 * k : 4 * k + 4, :, :rows].reshape(own.shape[1], 2 * width)
        for side, block in enumerate((own, other)):
            term = dot(block[...], panel, 1, 0).astype(BF)
            for part in range(2):
                out[2 * of + k if second else k, part, side] = term[:, part * width : (part + 1) * width]
    cols = pl.ds(pl.multiple_of(yl * width, width), width)
    strip = zc.shape[0] // 8
    for p in range(8):
        zc[p * strip : (p + 1) * strip] = xbuf[slot_of(p, x), :, rows:, cols].reshape(strip, width)
    store.wait()


def half_kernel(blocks, kt, out):
    pad = out.shape[1]
    for q in range(4):
        acc = None
        for o in range(kt.shape[0]):
            term = dot(blocks[o, q, :pad], kt[o], 1, 0)
            acc = term if acc is None else acc + term
        for o in range(kt.shape[0]):
            out[4 * o + 2 * (q % 2) + q // 2] = acc.astype(BF)


ANY = pl.BlockSpec(memory_space=pl.ANY)
SMEM = pl.BlockSpec(memory_space=pltpu.SMEM)
VM = pl.BlockSpec(memory_space=pltpu.VMEM)


def inner_call(own, other, ring, before=None):
    rows, k = own.shape
    deep, width = ring[0].shape[1:]
    second = before is not None
    count = 4 if second else 2
    return pl.pallas_call(
        functools.partial(inner_kernel, second),
        out_shape=(
            jax.ShapeDtypeStruct((count, 2, 2, rows, width // 2), BF),
            jax.ShapeDtypeStruct((16 * (deep - rows), width // 2), BF),
            jax.ShapeDtypeStruct((8, 2, rows, width), BF),
        ),
        in_specs=[VM, VM] + [VM] * 8 + [VM] * second,
        out_specs=(VM, VM, ANY),
        scratch_shapes=[
            pltpu.VMEM((8, 2, deep, width), BF),
            pltpu.SemaphoreType.DMA((8,)),
            pltpu.SemaphoreType.DMA,
        ],
        compiler_params=pltpu.CompilerParams(vmem_limit_bytes=VMEM),
        cost_estimate=pl.CostEstimate(flops=8 * rows * k * width, bytes_accessed=6 * 2**20, transcendentals=0),
        name="inner",
    )(own, other, *ring, *([before] if second else []))


def half_call(blocks, kt, pad):
    width = kt.shape[2]
    return pl.pallas_call(
        half_kernel,
        out_shape=jax.ShapeDtypeStruct((16, pad, width), BF),
        in_specs=[VM] * 2,
        out_specs=VM,
        compiler_params=pltpu.CompilerParams(vmem_limit_bytes=VMEM),
        cost_estimate=pl.CostEstimate(flops=8 * pad * 2048 * width, bytes_accessed=5 * 2**20, transcendentals=0),
        name="half",
    )(blocks, kt)


def sigma_kernel(scale, rows, h, near0, near1, far0, far1, out):
    yl, c = lax.axis_index("yl"), lax.axis_index("c")
    pad, width = h.shape[1:]
    acc = None
    for i, x in enumerate((near0, near1, far0, far1)):
        for k in range(2):
            at = 4 * (2 * (yl if i % 2 == 0 else 1 - yl) + k) + 2 * (c if i < 2 else 1 - c)
            a = jnp.concatenate([h[at], h[at + 1]], axis=1)
            term = dot(x[4 * k : 4 * k + 4].reshape(-1, 2 * width), a, 1, 1)
            acc = term if acc is None else acc + term
    acc = (acc * scale).T
    acc = jnp.concatenate([acc[:, b * pad : b * pad + rows] for b in range(acc.shape[1] // pad)], axis=1)
    out[...] = acc[:rows].astype(BF)


def sigma_call(h, near, far, rows, scale):
    pad = h.shape[1]
    width = near[0].shape[3]
    return pl.pallas_call(
        functools.partial(sigma_kernel, scale, rows),
        out_shape=jax.ShapeDtypeStruct((rows, 8 * rows), BF),
        in_specs=[VM] * 5,
        out_specs=VM,
        compiler_params=pltpu.CompilerParams(vmem_limit_bytes=VMEM),
        cost_estimate=pl.CostEstimate(flops=128 * pad * pad * width, bytes_accessed=8 * 2**20, transcendentals=0),
        name="sigma",
    )(h, *near, *far)


def local(green, colloc, core):
    nx = lax.axis_size("orb")
    c, x, tau, yl, z = (lax.axis_index(a) for a in ("c", "orb", "tau", "yl", "z"))
    rows, cols = colloc.shape
    pad = 192
    deep = pad + core.shape[0]
    half_cols = cols // 2
    quarter = cols // 4

    xpad = jnp.pad(colloc, ((0, pad - rows), (0, 0)))
    same, cross = [], []
    for i in range(32):
        for o in range(nx):
            a = i % 8
            if (i // 8 - o) % 2:
                a = 2 * (3 - a // 2) + a % 2
            to = o * 8 + a
            same.append((i * nx + o, to * nx + i // 8))
            cross.append((i * nx + o, (to ^ 1) * nx + i // 8))

    def halves(value):
        low, high = value[:, :half_cols], value[:, half_cols:]
        return jnp.where(c == 0, low, high), jnp.where(c == 0, high, low)

    stay, go = halves(xpad)
    stay = lax.ppermute(stay, GRID + ("orb",), same)
    go = lax.ppermute(go, GRID + ("orb",), cross)
    zstay, zgo = halves(core)
    zgo = shift(zgo, "c", 1)
    stay, go = jnp.concatenate([stay, zstay]), jnp.concatenate([go, zgo])
    own = jnp.where(c == 0, jnp.stack([stay, go]), jnp.stack([go, stay]))

    tile = green[0]
    blocks = tile.shape[1] // rows
    g_own = jnp.pad(tile.reshape(rows, blocks, rows), ((0, pad - rows), (0, 0), (0, pad - rows)))
    g_own = g_own.reshape(pad, blocks * pad)
    own, g_own = lax.optimization_barrier((own, g_own))
    g_other = shift(g_own, "c", 1)

    one_way, other_way = [(0, 2), (2, 0), (1, 3), (3, 1)], [(0, 3), (3, 0), (1, 2), (2, 1)]

    def across(value, way):
        return lax.ppermute(value, ("yl", "tau"), way)

    up, down, mate_up, mate_down = [own], [own], [], []
    for d in range(4):
        moved = [shift(up[d], "z", 1), across(up[d], one_way)]
        if d > 0:
            moved.append(across(down[d], other_way))
        if d < 3:
            moved.append(shift(down[d], "z", -1))
        moved = lax.optimization_barrier(moved)
        up.append(moved[0])
        mate_up.append(moved[1])
        if d > 0:
            mate_down.append(moved[2])
        if d < 3:
            down.append(moved[-1])
    mate_up.append(across(up[4], other_way))
    ring, mate = up + down[1:], mate_up + mate_down

    tall = jnp.concatenate([xpad, core])
    tall, _ = lax.optimization_barrier((tall, up[2]))
    tall = lax.all_gather(tall, ("orb", "yl", "c"), axis=0, tiled=False)
    tall = tall.reshape(nx, 4, deep, cols)

    inner, zfirst, near0 = inner_call(g_own, g_other, ring)
    inner, zsecond, near1 = inner_call(g_own, g_other, mate, inner)
    zcols = jnp.where(yl == 0, jnp.stack([zfirst, zsecond]), jnp.stack([zsecond, zfirst]))
    zcols = zcols.reshape(nx * cols, quarter)
    near = [near0, near1]
    far = [shift(v, "c", 1) for v in near]

    inner = swap(inner.reshape(8, 2, pad, quarter), ("orb", "yl")).reshape(nx, 2, 2, pad, quarter)
    inner = jnp.sum(inner.astype(F32), axis=0).astype(BF)
    inner = jnp.where(c == 0, inner, inner[:, ::-1])
    inner = jnp.pad(inner, ((0, 0), (0, 0), (0, deep - pad), (0, 0))).reshape(4 * deep, quarter)

    stack = tall.reshape(nx, 4 * deep, cols)
    part = lax.dot_general(stack, inner, (((1,), (0,)), ((), ())), preferred_element_type=F32)
    part = part.astype(BF).reshape(16, quarter, quarter)
    got = swap(part, ("tau", "z"))
    g = jnp.sum(got.reshape(2, 8, quarter, quarter).astype(F32), axis=1).astype(BF)
    gf = g.astype(F32)
    pair = (gf[0] * gf[1]).astype(BF)
    prow = spread(pair, ("orb", "c", "yl"))
    prow = jnp.transpose(prow, (1, 0, 2)).reshape(quarter, 16 * quarter)
    left = dot(prow, zcols, 1, 0).astype(BF)
    left = spread(left, ("tau", "z")).reshape(16 * quarter, quarter)
    zr = lax.dynamic_slice_in_dim(tall[:, :, pad:], 2 * tau, 2, 1)
    zr = jnp.transpose(zr, (1, 2, 0, 3)).reshape(quarter, nx * cols)
    screened = dot(zr, left, 1, 0)
    kern = (gf * screened[None]).astype(BF)
    kt = jnp.broadcast_to(kern[:, None], (2, 8, quarter, quarter)).reshape(16, quarter, quarter)
    kt = swap(kt, ("tau", "z")).reshape(nx, cols, quarter)
    hrow = swap(half_call(tall, kt, pad), ("orb", "c", "yl"))
    return sigma_call(hrow, near, far, rows, -1.0 / (nx * cols))[None]


def solution(mesh):
    fine = Mesh(mesh.devices.reshape(2, 8, 2, 4, 2), GRID + ("orb", "tau"))
    placed = (P("tau", GRID, "orb"), P(GRID, "orb"), P(GRID, "orb"))
    return jax.shard_map(
        local, mesh=fine, in_specs=placed, out_specs=P("tau", GRID, "orb"), check_vma=False
    )
```

```python
import functools

import jax
import jax.numpy as jnp
from jax import lax
from jax.experimental import pallas as pl
from jax.experimental.pallas import tpu as pltpu
from jax.sharding import Mesh
from jax.sharding import PartitionSpec as P

GRID = ("yl", "z", "c")
BF = jnp.bfloat16
F32 = jnp.float32
VMEM = 56 * 2**20


def swap(value, axes):
    return lax.all_to_all(value, axes, 0, 0, tiled=True)


def spread(value, axes):
    n = lax.axis_size(axes)
    return swap(jnp.broadcast_to(value[None], (n,) + value.shape), axes)


def shift(value, axis, by):
    n = lax.axis_size(axis)
    return lax.ppermute(value, axis, [(i, (i + by) % n) for i in range(n)])


def dot(a, b, ca, cb):
    return lax.dot_general(a, b, (((ca,), (cb,)), ((), ())), preferred_element_type=F32)


def fetch(pairs, sems):
    copies = [pltpu.make_async_copy(s, d, sems.at[i]) for i, (s, d) in enumerate(pairs)]
    for copy in copies:
        copy.start()
    return copies


def ring_places(z, n):
    return [z] + [lax.rem(z - d + n, n) for d in (1, 2, 3, 4)] + [lax.rem(z + d, n) for d in (1, 2, 3)]


def slot_of(p, x):
    return jnp.where(lax.div(p, 4) == lax.rem(x, 2), p, 4 * lax.div(p, 4) + 3 - lax.rem(p, 4))


def inner_kernel(second, own, other, *refs):
    ring, refs = refs[:8], refs[8:]
    if second:
        before, refs = refs[0], refs[1:]
    out, zc, rows_out, xbuf, xsem, osem = refs
    x, yl, z = (lax.axis_index(a) for a in ("orb", "yl", "z"))
    of = 1 - yl if second else yl
    copies = fetch([(r, xbuf.at[slot_of(p, x)]) for r, p in zip(ring, ring_places(z, 8))], xsem)
    if second:
        for k in range(2):
            out[2 * yl + k] = before[k]
    for copy in copies:
        copy.wait()
    rows, width = own.shape[0], out.shape[4]
    store = pltpu.make_async_copy(xbuf.at[:, :, pl.ds(0, rows)], rows_out, osem)
    store.start()
    for k in range(2):
        panel = xbuf[4 * k : 4 * k + 4, :, :rows].reshape(own.shape[1], 2 * width)
        for side, block in enumerate((own, other)):
            term = dot(block[...], panel, 1, 0).astype(BF)
            for part in range(2):
                out[2 * of + k if second else k, part, side] = term[:, part * width : (part + 1) * width]
    cols = pl.ds(pl.multiple_of(yl * width, width), width)
    strip = zc.shape[0] // 8
    for p in range(8):
        zc[p * strip : (p + 1) * strip] = xbuf[slot_of(p, x), :, rows:, cols].reshape(strip, width)
    store.wait()


def half_kernel(blocks, kt, out):
    pad = out.shape[1]
    for q in range(4):
        acc = None
        for o in range(kt.shape[0]):
            term = dot(blocks[o, q, :pad], kt[o], 1, 0)
            acc = term if acc is None else acc + term
        for o in range(kt.shape[0]):
            out[4 * o + 2 * (q % 2) + q // 2] = acc.astype(BF)


ANY = pl.BlockSpec(memory_space=pl.ANY)
SMEM = pl.BlockSpec(memory_space=pltpu.SMEM)
VM = pl.BlockSpec(memory_space=pltpu.VMEM)


def inner_call(own, other, ring, before=None):
    rows, k = own.shape
    deep, width = ring[0].shape[1:]
    second = before is not None
    count = 4 if second else 2
    return pl.pallas_call(
        functools.partial(inner_kernel, second),
        out_shape=(
            jax.ShapeDtypeStruct((count, 2, 2, rows, width // 2), BF),
            jax.ShapeDtypeStruct((16 * (deep - rows), width // 2), BF),
            jax.ShapeDtypeStruct((8, 2, rows, width), BF),
        ),
        in_specs=[VM, VM] + [VM] * 8 + [VM] * second,
        out_specs=(VM, VM, ANY),
        scratch_shapes=[
            pltpu.VMEM((8, 2, deep, width), BF),
            pltpu.SemaphoreType.DMA((8,)),
            pltpu.SemaphoreType.DMA,
        ],
        compiler_params=pltpu.CompilerParams(vmem_limit_bytes=VMEM),
        cost_estimate=pl.CostEstimate(flops=8 * rows * k * width, bytes_accessed=6 * 2**20, transcendentals=0),
        name="inner",
    )(own, other, *ring, *([before] if second else []))


def half_call(blocks, kt, pad):
    width = kt.shape[2]
    return pl.pallas_call(
        half_kernel,
        out_shape=jax.ShapeDtypeStruct((16, pad, width), BF),
        in_specs=[VM] * 2,
        out_specs=VM,
        compiler_params=pltpu.CompilerParams(vmem_limit_bytes=VMEM),
        cost_estimate=pl.CostEstimate(flops=8 * pad * 2048 * width, bytes_accessed=5 * 2**20, transcendentals=0),
        name="half",
    )(blocks, kt)


def sigma_kernel(scale, rows, h, near0, near1, far0, far1, out):
    yl, c = lax.axis_index("yl"), lax.axis_index("c")
    pad, width = h.shape[1:]
    acc = None
    for i, x in enumerate((near0, near1, far0, far1)):
        for k in range(2):
            at = 4 * (2 * (yl if i % 2 == 0 else 1 - yl) + k) + 2 * (c if i < 2 else 1 - c)
            a = jnp.concatenate([h[at], h[at + 1]], axis=1)
            term = dot(x[4 * k : 4 * k + 4].reshape(-1, 2 * width), a, 1, 1)
            acc = term if acc is None else acc + term
    acc = (acc * scale).T
    acc = jnp.concatenate([acc[:, b * pad : b * pad + rows] for b in range(acc.shape[1] // pad)], axis=1)
    out[...] = acc[:rows].astype(BF)


def sigma_call(h, near, far, rows, scale):
    pad = h.shape[1]
    width = near[0].shape[3]
    return pl.pallas_call(
        functools.partial(sigma_kernel, scale, rows),
        out_shape=jax.ShapeDtypeStruct((rows, 8 * rows), BF),
        in_specs=[VM] * 5,
        out_specs=VM,
        compiler_params=pltpu.CompilerParams(vmem_limit_bytes=VMEM),
        cost_estimate=pl.CostEstimate(flops=128 * pad * pad * width, bytes_accessed=8 * 2**20, transcendentals=0),
        name="sigma",
    )(h, *near, *far)


def local(green, colloc, core):
    nx = lax.axis_size("orb")
    c, x, tau, yl, z = (lax.axis_index(a) for a in ("c", "orb", "tau", "yl", "z"))
    rows, cols = colloc.shape
    pad = 192
    deep = pad + core.shape[0]
    half_cols = cols // 2
    quarter = cols // 4

    xpad = jnp.pad(colloc, ((0, pad - rows), (0, 0)))
    same, cross = [], []
    for i in range(32):
        for o in range(nx):
            a = i % 8
            if (i // 8 - o) % 2:
                a = 2 * (3 - a // 2) + a % 2
            to = o * 8 + a
            same.append((i * nx + o, to * nx + i // 8))
            cross.append((i * nx + o, (to ^ 1) * nx + i // 8))

    def halves(value):
        low, high = value[:, :half_cols], value[:, half_cols:]
        return jnp.where(c == 0, low, high), jnp.where(c == 0, high, low)

    stay, go = halves(xpad)
    stay = lax.ppermute(stay, GRID + ("orb",), same)
    go = lax.ppermute(go, GRID + ("orb",), cross)
    zstay, zgo = halves(core)
    zgo = shift(zgo, "c", 1)
    stay, go = jnp.concatenate([stay, zstay]), jnp.concatenate([go, zgo])
    own = jnp.where(c == 0, jnp.stack([stay, go]), jnp.stack([go, stay]))

    tile = green[0]
    blocks = tile.shape[1] // rows
    g_own = jnp.pad(tile.reshape(rows, blocks, rows), ((0, pad - rows), (0, 0), (0, pad - rows)))
    g_own = g_own.reshape(pad, blocks * pad)
    own, g_own = lax.optimization_barrier((own, g_own))
    g_other = shift(g_own, "c", 1)

    one_way, other_way = [(0, 2), (2, 0), (1, 3), (3, 1)], [(0, 3), (3, 0), (1, 2), (2, 1)]

    def across(value, way):
        return lax.ppermute(value, ("yl", "tau"), way)

    up, down, mate_up, mate_down = [own], [own], [], []
    for d in range(4):
        moved = [shift(up[d], "z", 1), across(up[d], one_way)]
        if d > 0:
            moved.append(across(down[d], other_way))
        if d < 3:
            moved.append(shift(down[d], "z", -1))
        if d < 3:
            moved = lax.optimization_barrier(moved)
        up.append(moved[0])
        mate_up.append(moved[1])
        if d > 0:
            mate_down.append(moved[2])
        if d < 3:
            down.append(moved[-1])
    mate_up.append(across(up[4], other_way))
    ring, mate = up + down[1:], mate_up + mate_down

    tall = jnp.concatenate([xpad, core])
    tall, _ = lax.optimization_barrier((tall, up[2]))
    tall = lax.all_gather(tall, ("orb", "yl", "c"), axis=0, tiled=False)
    tall = tall.reshape(nx, 4, deep, cols)

    inner, zfirst, near0 = inner_call(g_own, g_other, ring)
    inner, zsecond, near1 = inner_call(g_own, g_other, mate, inner)
    zcols = jnp.where(yl == 0, jnp.stack([zfirst, zsecond]), jnp.stack([zsecond, zfirst]))
    zcols = zcols.reshape(nx * cols, quarter)
    near = [near0, near1]
    far = [shift(v, "c", 1) for v in near]

    inner = swap(inner.reshape(8, 2, pad, quarter), ("orb", "yl")).reshape(nx, 2, 2, pad, quarter)
    inner = jnp.sum(inner.astype(F32), axis=0).astype(BF)
    inner = jnp.where(c == 0, inner, inner[:, ::-1])
    inner = jnp.pad(inner, ((0, 0), (0, 0), (0, deep - pad), (0, 0))).reshape(4 * deep, quarter)

    stack = tall.reshape(nx, 4 * deep, cols)
    part = lax.dot_general(stack, inner, (((1,), (0,)), ((), ())), preferred_element_type=F32)
    part = part.astype(BF).reshape(16, quarter, quarter)
    got = swap(part, ("tau", "z"))
    g = jnp.sum(got.reshape(2, 8, quarter, quarter).astype(F32), axis=1).astype(BF)
    gf = g.astype(F32)
    pair = (gf[0] * gf[1]).astype(BF)
    prow = spread(pair, ("orb", "c", "yl"))
    prow = jnp.transpose(prow, (1, 0, 2)).reshape(quarter, 16 * quarter)
    left = dot(prow, zcols, 1, 0).astype(BF)
    left = spread(left, ("tau", "z")).reshape(16 * quarter, quarter)
    zr = lax.dynamic_slice_in_dim(tall[:, :, pad:], 2 * tau, 2, 1)
    zr = jnp.transpose(zr, (1, 2, 0, 3)).reshape(quarter, nx * cols)
    screened = dot(zr, left, 1, 0)
    kern = (gf * screened[None]).astype(BF)
    kt = jnp.broadcast_to(kern[:, None], (2, 8, quarter, quarter)).reshape(16, quarter, quarter)
    kt = swap(kt, ("tau", "z")).reshape(nx, cols, quarter)
    hrow = swap(half_call(tall, kt, pad), ("orb", "c", "yl"))
    return sigma_call(hrow, near, far, rows, -1.0 / (nx * cols))[None]


def solution(mesh):
    fine = Mesh(mesh.devices.reshape(2, 8, 2, 4, 2), GRID + ("orb", "tau"))
    placed = (P("tau", GRID, "orb"), P(GRID, "orb"), P(GRID, "orb"))
    return jax.shard_map(
        local, mesh=fine, in_specs=placed, out_specs=P("tau", GRID, "orb"), check_vma=False
    )
```
